32 devices in a mesh: parts: 2 (over y), dp: 4 (over z), mp: 2 (over x), sub: 2 (over core).
Axes of the slice: x: 2, y: 2, z: 4, core: 2. Of those that a mesh axis runs over, the one named last changes fastest.
Arguments:
- activations: bfloat16 [2048, 5120], P(('parts', 'dp'), 'mp'), parts along dimension 0, may hold values from -6 to 6
- grads: bfloat16 [2048, 20480], P(('parts', 'dp'), 'mp'), parts along dimension 0, may hold values from -6 to 6
- act_basis: bfloat16 [5120, 2560], P('mp', 'sub'), may hold values from -0.078125 to 0.078125
- grad_basis: bfloat16 [20480, 1280], P(('mp', 'dp'), 'sub'), may hold values from -0.125 to 0.125
- doc_lengths: int32 [8, 4], P(('parts', 'dp')), parts along dimension 0, may hold values from 0 to 256, as said below
- owners: int32 [4], replicated, may hold values from 0 to 3, each once
Outputs:
- corrections: float32 [20480, 2560], P(('parts', 'mp', 'dp'), 'sub'), parts along dimension 0
The draws below stay inside these ranges and needn't reach their ends.
There are 2 independent parts, one for each index of `parts`. The reference program is written for one: setup_inputs(seed, part) draws one part's arguments, and reference() takes and returns one part's arrays. A program takes and returns all parts, laid end to end along the dimension named above; an argument that names none is the same for every part. Nothing has to cross between parts.
Inputs may be any that keep to these rules, and one draw needn't show every extreme that they name: `doc_lengths`: each row lists one window's documents: positive lengths in its first slots, zeros after them, summing to 256; some window holds 4 documents, and some window one document of 256 tokens. `owners`: every block index appears once.
All inputs are finite; a program needn't handle non-finite values.
Results may differ from the reference program's by a relative error of at most 0.012.
Values may be sent and summed in bfloat16 or wider, within the bound.
A program may use at most 256 MiB of HBM per device.

```python
import jax
import jax.numpy as jnp
from jax import lax

D = 5120
F = 20480
BG = 2560
GE = 1280
DE = 2560
TOK_DEV = 256
MAXDOC = 4
TOKENS = 1024
FE = 10240
ROWBLK = 1280
N_DP = 4
N_MP = 2


def draw_doc_lengths(key, part):
    key = jax.random.fold_in(key, 11)
    count_key, order_key, split_key = jax.random.split(key, 3)
    counts = jax.random.randint(count_key, (N_DP,), 1, MAXDOC + 1)
    window_order = jax.random.permutation(order_key, N_DP)
    counts = jnp.where(window_order == 0, MAXDOC, counts)
    counts = jnp.where(window_order == 1, 1, counts)
    window_keys = jax.random.split(split_key, N_DP)

    def one_window(window_key, doc_count):
        cut_points = jax.random.permutation(window_key, TOK_DEV - 1)[:MAXDOC - 1] + 1
        slot_ids = jnp.arange(MAXDOC - 1)
        cut_points = jnp.where(slot_ids < doc_count - 1, cut_points, TOK_DEV)
        cut_points = jnp.sort(cut_points)
        edges = jnp.concatenate([jnp.zeros((1,), jnp.int32), cut_points.astype(jnp.int32), jnp.full((1,), TOK_DEV, jnp.int32)])
        return edges[1:] - edges[:-1]
    return jax.vmap(one_window)(window_keys, counts).astype(jnp.int32)


def steps_of(own_key, extent, shards, smallest, high):
    def one(dim, shards_of):
        draws = jax.random.uniform(jax.random.fold_in(jax.random.fold_in(own_key, 6), dim), (shards_of,), jnp.float32, smallest / len(shards), high / len(shards))
        return jnp.repeat(jnp.exp(draws), extent[dim] // shards_of).reshape((-1,) + (1,) * (len(extent) - dim - 1))

    factor_of = one(*shards[0])
    for cut in shards[1:]:
        factor_of = factor_of * one(*cut)
    return factor_of


def bell_draw(own_key, shape, width, limit, cuts=(), kind=jnp.bfloat16):
    drawn = width * jax.random.normal(own_key, shape, jnp.float32)
    if cuts:
        drawn = drawn * steps_of(own_key, shape, cuts, -0.22, 0.18)
    return jnp.clip(drawn, -limit, limit).astype(kind)


def setup_inputs(seed: int = 0, part: int = 0) -> dict:
    keys = jax.random.split(jax.random.key(seed), 7)
    part_splits = jax.random.split(jax.random.fold_in(keys[6], part), 7)
    activations = bell_draw(part_splits[0], (TOKENS, D), 1.0, 6.0, ((0, 4), (1, 2)))
    grads = bell_draw(part_splits[1], (TOKENS, F), 1.0, 6.0, ((0, 4), (1, 2)))
    act_basis = bell_draw(keys[2], (D, DE), D ** -0.5, 0.078125, ((0, 2), (1, 2)))
    grad_basis = bell_draw(keys[3], (F, GE), BG ** -0.5, 0.125, ((0, 8), (1, 2)))
    doc_lengths = draw_doc_lengths(jax.random.fold_in(jax.random.fold_in(keys[6], part), 71), part)
    owners = jax.random.permutation(keys[5], N_DP).astype(jnp.int32)
    return dict(activations=activations, grads=grads, act_basis=act_basis, grad_basis=grad_basis, doc_lengths=doc_lengths, owners=owners)


def window_terms(grad_rows, act_rows, slot_ids):
    window_total = jnp.zeros((grad_rows.shape[1], act_rows.shape[1]), jnp.float32)
    for slot_index in range(MAXDOC):
        keep_mask = (slot_ids == slot_index).astype(jnp.float32)
        masked = act_rows * keep_mask[:, None]
        product = lax.dot_general(grad_rows, masked, (((0,), (0,)), ((), ())), precision=lax.Precision.HIGHEST, preferred_element_type=jnp.float32)
        window_total = window_total + product * product
    return window_total


def reference(activations, grads, act_basis, grad_basis, doc_lengths, owners):
    block_count = F // BG
    act_rot = jnp.dot(activations, act_basis, preferred_element_type=jnp.float32).astype(jnp.bfloat16)
    grad_blocks = grads.reshape(TOKENS, block_count, BG).astype(jnp.float32)
    basis_blocks = grad_basis.reshape(block_count, BG, GE).astype(jnp.float32)
    grad_rot = jnp.einsum("tbk,bke->tbe", grad_blocks, basis_blocks, precision=lax.Precision.HIGHEST)
    grad_rot = grad_rot.reshape(TOKENS, FE).astype(jnp.bfloat16)
    ends = jnp.cumsum(doc_lengths, axis=1).astype(jnp.int32)
    positions = jnp.arange(TOK_DEV, dtype=jnp.int32)

    def one_window(running, window_index):
        first_row = (window_index * TOK_DEV).astype(jnp.int32)
        grad_rows = lax.dynamic_slice_in_dim(grad_rot, first_row, TOK_DEV, 0).astype(jnp.float32)
        act_rows = lax.dynamic_slice_in_dim(act_rot, first_row, TOK_DEV, 0).astype(jnp.float32)
        end_row = lax.dynamic_index_in_dim(ends, window_index, 0, keepdims=False)
        slot_ids = jnp.sum((positions[:, None] >= end_row[None, :]).astype(jnp.int32), axis=1)
        window_total = window_terms(grad_rows, act_rows, slot_ids)
        rounded = lax.optimization_barrier(window_total.astype(jnp.bfloat16))
        return running + rounded.astype(jnp.float32), None

    summed, unused = lax.scan(one_window, jnp.zeros((FE, DE), jnp.float32), jnp.arange(N_DP, dtype=jnp.int32))
    scaled = summed / TOKENS
    owner_ids = jnp.arange(N_DP, dtype=jnp.int32)
    inverse = jnp.sum(owner_ids[:, None] * (owners[:, None] == owner_ids[None, :]).astype(jnp.int32), axis=0)
    grouped = scaled.reshape(N_MP, N_DP, ROWBLK, DE)
    return jnp.take(grouped, inverse, axis=1).reshape(FE, DE)
```

```python
import itertools

import jax
import jax.numpy as jnp
from jax import lax
from jax.experimental import pallas as pl
from jax.experimental.pallas import tpu as pltpu
from jax.sharding import PartitionSpec as P

BG = 2560
MAXDOC = 4


def rotate_piece(grads, running, shard_rows):
    row_count = shard_rows.shape[0]
    block_count = running.shape[1]
    block_of = jnp.arange(row_count, dtype=jnp.int32) // BG
    pieces = []
    for block_index in range(block_count):
        keep_mask = (block_of == block_index).astype(grads.dtype)
        pieces.append(
            jnp.dot(grads * keep_mask[None, :], shard_rows, preferred_element_type=jnp.float32)
        )
    return jnp.stack(pieces, axis=1)


def window_squares(grad_rows, act_rows, slot_ids):
    window_total = jnp.zeros((grad_rows.shape[1], act_rows.shape[1]), jnp.float32)
    for slot_index in range(MAXDOC):
        masked = act_rows * (slot_ids == slot_index).astype(act_rows.dtype)[:, None]
        product = lax.dot_general(
            grad_rows, masked, (((0,), (0,)), ((), ())), preferred_element_type=jnp.float32
        )
        window_total = window_total + product * product
    return window_total


def inverse_of(owners, dp_count):
    owner_ids = jnp.arange(dp_count, dtype=jnp.int32)
    return jnp.sum(
        owner_ids[:, None] * (owners[:, None] == owner_ids[None, :]).astype(jnp.int32), axis=0
    )


def general_shards(activations, grads, act_basis, grad_basis, doc_lengths, owners):
    tok_rows = grads.shape[0]
    block_count = grads.shape[1] // BG
    act_partial = jnp.dot(activations, act_basis, preferred_element_type=jnp.float32)
    act_rot = lax.psum(act_partial.astype(jnp.bfloat16), "mp")
    start_sum = jnp.zeros((tok_rows, block_count, grad_basis.shape[1]), jnp.float32)
    half_rot = rotate_piece(
        grads, start_sum, lax.all_gather(grad_basis, "dp", axis=0, tiled=True)
    ).astype(jnp.bfloat16)
    grad_rot = lax.all_gather(half_rot, "sub", axis=2, tiled=True)
    grad_flat = grad_rot.reshape(tok_rows, block_count * grad_rot.shape[2])
    ends = jnp.cumsum(doc_lengths[0])
    positions = jnp.arange(tok_rows, dtype=jnp.int32)
    doc_slot = jnp.sum((positions[:, None] >= ends[None, :]).astype(jnp.int32), axis=1)
    dp_count = lax.axis_size("dp")
    inverse = inverse_of(owners, dp_count)
    row_block = grad_flat.shape[1] // dp_count
    ordered_cols = jnp.take(grad_flat.reshape(tok_rows, dp_count, row_block), inverse, axis=1)
    ordered_cols = ordered_cols.reshape(tok_rows, dp_count * row_block)
    total_tokens = tok_rows * dp_count
    window_total = window_squares(ordered_cols, act_rot, doc_slot)
    summed = lax.psum_scatter(
        window_total.astype(jnp.bfloat16), "dp", scatter_dimension=0, tiled=True
    ).astype(jnp.float32)
    return summed / total_tokens


def squares_kernel(total_tokens, ends_ref, g_ref, a_ref, o_ref, total):
    window_count, tok_rows, row_count = g_ref.shape
    col_count = a_ref.shape[2]
    step = 256
    token = lax.broadcasted_iota(jnp.int32, (1, tok_rows), 1)
    for window in range(window_count):
        flipped = g_ref[window].astype(jnp.float32).T
        for slot in range(MAXDOC):
            first = 0 if slot == 0 else ends_ref[window, slot - 1]
            last = ends_ref[window, slot]

            def one_slot():
                keep = ((token >= first) & (token < last)).astype(jnp.float32)
                masked = (flipped * keep).astype(jnp.bfloat16)
                for col in range(0, col_count, step):
                    product = jnp.dot(
                        masked, a_ref[window, :, col:col + step], preferred_element_type=jnp.float32
                    )
                    if slot == 0:
                        total[:, col:col + step] = product * product
                    else:
                        total[:, col:col + step] += product * product

            if slot == 0:
                one_slot()
            else:
                pl.when(last > first)(one_slot)
        rounded = total[...].astype(jnp.bfloat16).astype(jnp.float32)
        if window == 0:
            o_ref[...] = rounded
        elif window < window_count - 1:
            o_ref[...] += rounded
        else:
            o_ref[...] = (o_ref[...] + rounded) / total_tokens


def owned_squares(ends, grad_rows, act_rows, total_tokens):
    window_count, tok_rows, row_count = grad_rows.shape
    col_count = act_rows.shape[2]
    tile = 256
    multiplies = window_count * MAXDOC * tok_rows * row_count * col_count
    return pl.pallas_call(
        lambda *refs: squares_kernel(total_tokens, *refs),
        grid=(row_count // tile,),
        out_shape=jax.ShapeDtypeStruct((row_count, col_count), jnp.float32),
        in_specs=[
            pl.BlockSpec(memory_space=pltpu.SMEM),
            pl.BlockSpec((window_count, tok_rows, tile), lambda i: (0, 0, i)),
            pl.BlockSpec((window_count, tok_rows, col_count), lambda i: (0, 0, 0)),
        ],
        out_specs=pl.BlockSpec((tile, col_count), lambda i: (i, 0)),
        scratch_shapes=[pltpu.VMEM((tile, col_count), jnp.float32)],
        compiler_params=pltpu.CompilerParams(vmem_limit_bytes=40 * 2**20),
        cost_estimate=pl.CostEstimate(
            flops=2 * multiplies,
            bytes_accessed=4 * row_count * col_count + 4 * window_count * tok_rows * col_count,
            transcendentals=0,
        ),
    )(ends, grad_rows, act_rows)


def to_owner(block, owners, dp_count):
    orders = list(itertools.permutations(range(dp_count)))
    table = jnp.array(orders, jnp.int32)
    which = jnp.argmax(jnp.all(table == owners[None, :], axis=1)).astype(jnp.int32)
    branches = [
        lambda moved, order=order: lax.ppermute(moved, "dp", [(j, order[j]) for j in range(dp_count)])
        for order in orders
    ]
    return lax.switch(which, branches, block)


def block_shards(activations, grads, act_basis, grad_basis, doc_lengths, owners):
    tok_rows = grads.shape[0]
    dp_count = lax.axis_size("dp")
    sub_count = lax.axis_size("sub")
    me = lax.axis_index("dp")
    half = tok_rows // sub_count
    basis = lax.all_gather(grad_basis, "sub", axis=1, tiled=True)
    first_row = lax.axis_index("sub") * half
    arrived = []
    for shift in range(dp_count):
        target = lax.rem(me + shift, dp_count)
        piece = lax.dynamic_slice(grads, (first_row, target * BG), (half, BG))
        if shift:
            piece = lax.ppermute(piece, "dp", [(i, (i + shift) % dp_count) for i in range(dp_count)])
        arrived.append(piece)
    act_partial = jnp.dot(activations, act_basis, preferred_element_type=jnp.float32)
    act_share = lax.psum_scatter(
        act_partial.astype(jnp.bfloat16), "mp", scatter_dimension=0, tiled=True
    )
    act_all = lax.all_gather(act_share, "dp", axis=0)
    act_all = lax.all_gather(act_all, "mp", axis=1, tiled=True)
    lengths = lax.all_gather(doc_lengths, "dp", axis=0, tiled=True)
    ends = jnp.cumsum(lengths, axis=1).astype(jnp.int32)
    rotated = [
        jnp.dot(piece, basis, preferred_element_type=jnp.float32).astype(jnp.bfloat16)
        for piece in arrived
    ]
    stacked = jnp.stack(rotated)
    windows = lax.rem(me - jnp.arange(dp_count, dtype=jnp.int32) + dp_count, dp_count)
    stacked = jnp.take(stacked, windows, axis=0)
    owned = to_owner(stacked, owners, dp_count)
    grad_all = lax.all_gather(owned, "sub", axis=1, tiled=True)
    return owned_squares(ends, grad_all, act_all, tok_rows * dp_count)


def shards(activations, grads, act_basis, grad_basis, doc_lengths, owners):
    whole_blocks = grad_basis.shape[0] == BG and grads.shape[1] == BG * lax.axis_size("dp")
    plan = block_shards if whole_blocks and lax.axis_size("dp") <= 4 else general_shards
    return plan(activations, grads, act_basis, grad_basis, doc_lengths, owners)


def solution(mesh):
    return jax.shard_map(
        shards,
        mesh=mesh,
        in_specs=(
            P(("parts", "dp"), "mp"),
            P(("parts", "dp"), "mp"),
            P("mp", "sub"),
            P(("mp", "dp"), "sub"),
            P(("parts", "dp"), None),
            P(),
        ),
        out_specs=P(("parts", "mp", "dp"), "sub"),
        check_vma=False,
    )
```

```python
import itertools

import jax
import jax.numpy as jnp
from jax import lax
from jax.experimental import pallas as pl
from jax.experimental.pallas import tpu as pltpu
from jax.sharding import PartitionSpec as P

BG = 2560
MAXDOC = 4


def rotate_piece(grads, running, shard_rows):
    row_count = shard_rows.shape[0]
    block_count = running.shape[1]
    block_of = jnp.arange(row_count, dtype=jnp.int32) // BG
    pieces = []
    for block_index in range(block_count):
        keep_mask = (block_of == block_index).astype(grads.dtype)
        pieces.append(
            jnp.dot(grads * keep_mask[None, :], shard_rows, preferred_element_type=jnp.float32)
        )
    return jnp.stack(pieces, axis=1)


def window_squares(grad_rows, act_rows, slot_ids):
    window_total = jnp.zeros((grad_rows.shape[1], act_rows.shape[1]), jnp.float32)
    for slot_index in range(MAXDOC):
        masked = act_rows * (slot_ids == slot_index).astype(act_rows.dtype)[:, None]
        product = lax.dot_general(
            grad_rows, masked, (((0,), (0,)), ((), ())), preferred_element_type=jnp.float32
        )
        window_total = window_total + product * product
    return window_total


def inverse_of(owners, dp_count):
    owner_ids = jnp.arange(dp_count, dtype=jnp.int32)
    return jnp.sum(
        owner_ids[:, None] * (owners[:, None] == owner_ids[None, :]).astype(jnp.int32), axis=0
    )


def general_shards(activations, grads, act_basis, grad_basis, doc_lengths, owners):
    tok_rows = grads.shape[0]
    block_count = grads.shape[1] // BG
    act_partial = jnp.dot(activations, act_basis, preferred_element_type=jnp.float32)
    act_rot = lax.psum(act_partial.astype(jnp.bfloat16), "mp")
    start_sum = jnp.zeros((tok_rows, block_count, grad_basis.shape[1]), jnp.float32)
    half_rot = rotate_piece(
        grads, start_sum, lax.all_gather(grad_basis, "dp", axis=0, tiled=True)
    ).astype(jnp.bfloat16)
    grad_rot = lax.all_gather(half_rot, "sub", axis=2, tiled=True)
    grad_flat = grad_rot.reshape(tok_rows, block_count * grad_rot.shape[2])
    ends = jnp.cumsum(doc_lengths[0])
    positions = jnp.arange(tok_rows, dtype=jnp.int32)
    doc_slot = jnp.sum((positions[:, None] >= ends[None, :]).astype(jnp.int32), axis=1)
    dp_count = lax.axis_size("dp")
    inverse = inverse_of(owners, dp_count)
    row_block = grad_flat.shape[1] // dp_count
    ordered_cols = jnp.take(grad_flat.reshape(tok_rows, dp_count, row_block), inverse, axis=1)
    ordered_cols = ordered_cols.reshape(tok_rows, dp_count * row_block)
    total_tokens = tok_rows * dp_count
    window_total = window_squares(ordered_cols, act_rot, doc_slot)
    summed = lax.psum_scatter(
        window_total.astype(jnp.bfloat16), "dp", scatter_dimension=0, tiled=True
    ).astype(jnp.float32)
    return summed / total_tokens


def squares_kernel(total_tokens, ends_ref, own_ref, other_ref, a_ref, o_ref, total):
    window_count, half, row_count = own_ref.shape
    tok_rows = a_ref.shape[1]
    is_first = lax.axis_index("sub") == 0
    col_count = a_ref.shape[2]
    step = 256
    token = lax.broadcasted_iota(jnp.int32, (1, tok_rows), 1)
    for window in range(window_count):
        own = own_ref[window].astype(jnp.float32)
        other = other_ref[window].astype(jnp.float32)
        rows = jnp.concatenate(
            [jnp.where(is_first, own, other), jnp.where(is_first, other, own)], axis=0
        )
        flipped = rows.T
        for slot in range(MAXDOC):
            first = 0 if slot == 0 else ends_ref[window, slot - 1]
            last = ends_ref[window, slot]

            def one_slot():
                keep = ((token >= first) & (token < last)).astype(jnp.float32)
                masked = (flipped * keep).astype(jnp.bfloat16)
                for col in range(0, col_count, step):
                    product = jnp.dot(
                        masked, a_ref[window, :, col:col + step], preferred_element_type=jnp.float32
                    )
                    if slot == 0:
                        total[:, col:col + step] = product * product
                    else:
                        total[:, col:col + step] += product * product

            if slot == 0:
                one_slot()
            else:
                pl.when(last > first)(one_slot)
        rounded = total[...].astype(jnp.bfloat16).astype(jnp.float32)
        if window == 0:
            o_ref[...] = rounded
        elif window < window_count - 1:
            o_ref[...] += rounded
        else:
            o_ref[...] = (o_ref[...] + rounded) / total_tokens


def owned_squares(ends, own_rows, other_rows, act_rows, total_tokens):
    window_count, half, row_count = own_rows.shape
    tok_rows = act_rows.shape[1]
    col_count = act_rows.shape[2]
    tile = 256
    multiplies = window_count * MAXDOC * tok_rows * row_count * col_count
    return pl.pallas_call(
        lambda *refs: squares_kernel(total_tokens, *refs),
        grid=(row_count // tile,),
        out_shape=jax.ShapeDtypeStruct((row_count, col_count), jnp.float32),
        in_specs=[
            pl.BlockSpec(memory_space=pltpu.SMEM),
            pl.BlockSpec((window_count, half, tile), lambda i: (0, 0, i)),
            pl.BlockSpec((window_count, half, tile), lambda i: (0, 0, i)),
            pl.BlockSpec((window_count, tok_rows, col_count), lambda i: (0, 0, 0)),
        ],
        out_specs=pl.BlockSpec((tile, col_count), lambda i: (i, 0)),
        scratch_shapes=[pltpu.VMEM((tile, col_count), jnp.float32)],
        compiler_params=pltpu.CompilerParams(vmem_limit_bytes=40 * 2**20),
        cost_estimate=pl.CostEstimate(
            flops=2 * multiplies,
            bytes_accessed=4 * row_count * col_count + 4 * window_count * tok_rows * col_count,
            transcendentals=0,
        ),
    )(ends, own_rows, other_rows, act_rows)


def exchange_kernel(
    dp_count, grads, basis, acts, act_basis, r_out, a_out,
    g_buf, b_buf, x_buf, w_buf, part, came, a_all, r_buf,
    g_send, g_recv, z_send, z_recv, x_send, x_recv, one_send, one_recv, local,
):
    me = lax.axis_index("dp")
    sub = lax.axis_index("sub")
    mp = lax.axis_index("mp")
    half = g_buf.shape[1]
    mesh_id = pl.DeviceIdType.MESH

    def to_dp(shift):
        return {"dp": lax.rem(me + shift, dp_count)}

    def from_dp(shift):
        return lax.rem(me + dp_count - shift, dp_count)

    to_mp = {"mp": 1 - mp}
    to_sub = {"sub": 1 - sub}

    own_copies = [
        pltpu.make_async_copy(acts, x_buf, local.at[0]),
        pltpu.make_async_copy(act_basis, w_buf, local.at[1]),
        pltpu.make_async_copy(basis, b_buf.at[sub], local.at[2]),
        pltpu.make_async_copy(
            grads.at[pl.ds(sub * half, half), pl.ds(me * BG, BG)], g_buf.at[me], local.at[3]
        ),
    ]
    for copy in own_copies:
        copy.start()

    barrier = pltpu.get_barrier_semaphore()
    for shift in range(1, dp_count):
        pl.semaphore_signal(barrier, inc=1, device_id=to_dp(shift), device_id_type=mesh_id)
    pl.semaphore_signal(barrier, inc=1, device_id=to_mp, device_id_type=mesh_id)
    pl.semaphore_signal(barrier, inc=1, device_id=to_sub, device_id_type=mesh_id)
    pl.semaphore_wait(barrier, dp_count + 1)

    def remote(src, dst, send, recv, target):
        return pltpu.make_async_remote_copy(
            src_ref=src, dst_ref=dst, send_sem=send, recv_sem=recv,
            device_id=target, device_id_type=mesh_id,
        )

    def grad_copy(shift):
        target = lax.rem(me + shift, dp_count)
        return remote(
            grads.at[pl.ds(sub * half, half), pl.ds(target * BG, BG)], g_buf.at[me],
            g_send.at[shift], g_recv.at[shift], to_dp(shift),
        )

    def grad_arrival(shift):
        return remote(
            g_buf.at[from_dp(shift)], g_buf.at[from_dp(shift)],
            g_send.at[shift], g_recv.at[shift], to_dp(shift),
        )

    basis_copy = remote(basis, b_buf.at[sub], one_send.at[0], one_recv.at[0], to_sub)
    basis_arrival = remote(basis, b_buf.at[1 - sub], one_send.at[0], one_recv.at[0], to_sub)
    grad_copies = [grad_copy(shift) for shift in range(1, dp_count)]
    for copy in grad_copies:
        copy.start()
    basis_copy.start()

    own_copies[0].wait()
    own_copies[1].wait()
    step = 256

    @pl.loop(0, w_buf.shape[1] // step)
    def _(index):
        cols = pl.ds(pl.multiple_of(index * step, step), step)
        product = jnp.dot(x_buf[...], w_buf[:, cols], preferred_element_type=jnp.float32)
        product = product.astype(jnp.bfloat16)
        part[0, :, cols] = product[:half]
        part[1, :, cols] = product[half:]

    share_copy = remote(part.at[1 - mp], came, one_send.at[1], one_recv.at[1], to_mp)
    share_copy.start()

    def rotate(window):
        width = b_buf.shape[2]
        piece = g_buf[window]
        for side in range(2):
            r_buf[window, :, side * width:(side + 1) * width] = jnp.dot(
                piece, b_buf[side], preferred_element_type=jnp.float32
            ).astype(jnp.bfloat16)

    share_copy.wait_recv()
    a_all[me, mp] = (
        part[mp].astype(jnp.float32) + came[...].astype(jnp.float32)
    ).astype(jnp.bfloat16)

    def act_copy(shift):
        return remote(
            a_all.at[me, mp], a_all.at[me, mp], z_send.at[shift], z_recv.at[shift], to_dp(shift)
        )

    def act_arrival(shift):
        window = from_dp(shift)
        return remote(
            a_all.at[window, mp], a_all.at[window, mp], z_send.at[shift], z_recv.at[shift], to_dp(shift)
        )

    def cross_copy(shift):
        window = from_dp(shift)
        return remote(
            a_all.at[window, mp], a_all.at[window, mp], x_send.at[shift], x_recv.at[shift], to_mp
        )

    def cross_arrival(shift):
        window = from_dp(shift)
        return remote(
            a_all.at[window, 1 - mp], a_all.at[window, 1 - mp], x_send.at[shift], x_recv.at[shift], to_mp
        )

    act_copies = [act_copy(shift) for shift in range(1, dp_count)]
    for copy in act_copies:
        copy.start()
    cross_copies = [cross_copy(shift) for shift in range(dp_count)]
    cross_copies[0].start()

    own_copies[2].wait()
    own_copies[3].wait()
    basis_arrival.wait_recv()
    rotate(me)
    for shift in (1, 3, 2):
        grad_arrival(shift).wait_recv()
        rotate(from_dp(shift))
    r_copy = pltpu.make_async_copy(r_buf, r_out, local.at[0])
    r_copy.start()
    for shift in (1, 3, 2):
        act_arrival(shift).wait_recv()
        cross_copies[shift].start()
    for shift in range(dp_count):
        cross_arrival(shift).wait_recv()
    a_copy = pltpu.make_async_copy(a_all, a_out, local.at[1])
    a_copy.start()
    basis_copy.wait_send()
    share_copy.wait_send()
    for copy in grad_copies + act_copies + cross_copies:
        copy.wait_send()
    r_copy.wait()
    a_copy.wait()


def exchange(activations, grads, act_basis, grad_basis):
    dp_count = lax.axis_size("dp")
    tok_rows = grads.shape[0]
    half = tok_rows // 2
    width = grad_basis.shape[1]
    cols = act_basis.shape[1]
    anywhere = pl.BlockSpec(memory_space=pl.ANY)
    dma = pltpu.SemaphoreType.DMA
    kind = jnp.bfloat16
    rotated, acts = pl.pallas_call(
        lambda *refs: exchange_kernel(dp_count, *refs),
        out_shape=(
            jax.ShapeDtypeStruct((dp_count, half, 2 * width), kind),
            jax.ShapeDtypeStruct((dp_count, 2, half, cols), kind),
        ),
        in_specs=[anywhere] * 4,
        out_specs=(anywhere, anywhere),
        scratch_shapes=[
            pltpu.VMEM((dp_count, half, BG), kind),
            pltpu.VMEM((2, BG, width), kind),
            pltpu.VMEM(activations.shape, kind),
            pltpu.VMEM(act_basis.shape, kind),
            pltpu.VMEM((2, half, cols), kind),
            pltpu.VMEM((half, cols), kind),
            pltpu.VMEM((dp_count, 2, half, cols), kind),
            pltpu.VMEM((dp_count, half, 2 * width), kind),
            dma((dp_count,)), dma((dp_count,)), dma((dp_count,)), dma((dp_count,)),
            dma((dp_count,)), dma((dp_count,)), dma((2,)), dma((2,)), dma((4,)),
        ],
        compiler_params=pltpu.CompilerParams(
            collective_id=0, has_side_effects=True, vmem_limit_bytes=40 * 2**20
        ),
        cost_estimate=pl.CostEstimate(flops=7 * 10**9, bytes_accessed=2**25, transcendentals=0),
    )(grads, grad_basis, activations, act_basis)
    return rotated, acts.reshape(dp_count, tok_rows, cols)


def to_owner(block, owners, dp_count):
    orders = list(itertools.permutations(range(dp_count)))
    table = jnp.array(orders, jnp.int32)
    which = jnp.argmax(jnp.all(table == owners[None, :], axis=1)).astype(jnp.int32)
    branches = [
        lambda moved, order=order: lax.ppermute(moved, "dp", [(j, order[j]) for j in range(dp_count)])
        for order in orders
    ]
    return lax.switch(which, branches, block)


def block_shards(activations, grads, act_basis, grad_basis, doc_lengths, owners):
    tok_rows = grads.shape[0]
    dp_count = lax.axis_size("dp")
    rotated, act_all = exchange(activations, grads, act_basis, grad_basis)
    lengths = lax.all_gather(doc_lengths, "dp", axis=0, tiled=True)
    ends = jnp.cumsum(lengths, axis=1).astype(jnp.int32)
    owned = to_owner(rotated, owners, dp_count)
    other = lax.ppermute(owned, "sub", [(0, 1), (1, 0)])
    return owned_squares(ends, owned, other, act_all, tok_rows * dp_count)


def shards(activations, grads, act_basis, grad_basis, doc_lengths, owners):
    whole_blocks = grad_basis.shape[0] == BG and grads.shape[1] == BG * lax.axis_size("dp")
    pairs = lax.axis_size("mp") == 2 and lax.axis_size("sub") == 2 and lax.axis_size("dp") == 4
    plan = block_shards if whole_blocks and pairs else general_shards
    return plan(activations, grads, act_basis, grad_basis, doc_lengths, owners)


def solution(mesh):
    return jax.shard_map(
        shards,
        mesh=mesh,
        in_specs=(
            P(("parts", "dp"), "mp"),
            P(("parts", "dp"), "mp"),
            P("mp", "sub"),
            P(("mp", "dp"), "sub"),
            P(("parts", "dp"), None),
            P(),
        ),
        out_specs=P(("parts", "mp", "dp"), "sub"),
        check_vma=False,
    )
```

```python
import itertools

import jax
import jax.numpy as jnp
from jax import lax
from jax.experimental import pallas as pl
from jax.experimental.pallas import tpu as pltpu
from jax.sharding import PartitionSpec as P

BG = 2560
MAXDOC = 4
VMEM_LIMIT = 60 * 2**20


def rotate_piece(grads, running, shard_rows):
    row_count = shard_rows.shape[0]
    block_count = running.shape[1]
    block_of = jnp.arange(row_count, dtype=jnp.int32) // BG
    pieces = []
    for block_index in range(block_count):
        keep_mask = (block_of == block_index).astype(grads.dtype)
        pieces.append(
            jnp.dot(grads * keep_mask[None, :], shard_rows, preferred_element_type=jnp.float32)
        )
    return jnp.stack(pieces, axis=1)


def window_squares(grad_rows, act_rows, slot_ids):
    window_total = jnp.zeros((grad_rows.shape[1], act_rows.shape[1]), jnp.float32)
    for slot_index in range(MAXDOC):
        masked = act_rows * (slot_ids == slot_index).astype(act_rows.dtype)[:, None]
        product = lax.dot_general(
            grad_rows, masked, (((0,), (0,)), ((), ())), preferred_element_type=jnp.float32
        )
        window_total = window_total + product * product
    return window_total


def inverse_of(owners, dp_count):
    owner_ids = jnp.arange(dp_count, dtype=jnp.int32)
    return jnp.sum(
        owner_ids[:, None] * (owners[:, None] == owner_ids[None, :]).astype(jnp.int32), axis=0
    )


def general_shards(activations, grads, act_basis, grad_basis, doc_lengths, owners):
    tok_rows = grads.shape[0]
    block_count = grads.shape[1] // BG
    act_partial = jnp.dot(activations, act_basis, preferred_element_type=jnp.float32)
    act_rot = lax.psum(act_partial.astype(jnp.bfloat16), "mp")
    start_sum = jnp.zeros((tok_rows, block_count, grad_basis.shape[1]), jnp.float32)
    half_rot = rotate_piece(
        grads, start_sum, lax.all_gather(grad_basis, "dp", axis=0, tiled=True)
    ).astype(jnp.bfloat16)
    grad_rot = lax.all_gather(half_rot, "sub", axis=2, tiled=True)
    grad_flat = grad_rot.reshape(tok_rows, block_count * grad_rot.shape[2])
    ends = jnp.cumsum(doc_lengths[0])
    positions = jnp.arange(tok_rows, dtype=jnp.int32)
    doc_slot = jnp.sum((positions[:, None] >= ends[None, :]).astype(jnp.int32), axis=1)
    dp_count = lax.axis_size("dp")
    inverse = inverse_of(owners, dp_count)
    row_block = grad_flat.shape[1] // dp_count
    ordered_cols = jnp.take(grad_flat.reshape(tok_rows, dp_count, row_block), inverse, axis=1)
    ordered_cols = ordered_cols.reshape(tok_rows, dp_count * row_block)
    total_tokens = tok_rows * dp_count
    window_total = window_squares(ordered_cols, act_rot, doc_slot)
    summed = lax.psum_scatter(
        window_total.astype(jnp.bfloat16), "dp", scatter_dimension=0, tiled=True
    ).astype(jnp.float32)
    return summed / total_tokens


def squares_kernel(total_tokens, lengths_ref, own_ref, other_ref, a_ref, o_ref):
    window_count = own_ref.shape[0]
    tok_rows, col_count = a_ref.shape[1:]
    step = 256
    is_first = lax.axis_index("sub") == 0
    token = lax.broadcasted_iota(jnp.int32, (1, tok_rows), 1)
    for window in range(window_count):
        own, other = own_ref[window], other_ref[window]
        rows = jnp.concatenate(
            [jnp.where(is_first, own, other), jnp.where(is_first, other, own)], axis=0
        )
        flipped = rows.T
        lengths = [lengths_ref[window, 0, slot] for slot in range(MAXDOC)]
        ends = [sum(lengths[1:slot + 1], lengths[0]) for slot in range(MAXDOC)]
        used = sum([(length > 0).astype(jnp.int32) for length in lengths[1:]], 1)

        def documents(count):
            pieces = []
            for slot in range(count):
                keep = token < ends[slot]
                if slot:
                    keep = keep & (token >= ends[slot - 1])
                pieces.append(flipped * keep.astype(jnp.float32).astype(flipped.dtype))
            for col in range(0, col_count, step):
                summed = None
                for piece in pieces:
                    product = jnp.dot(
                        piece, a_ref[window, :, col:col + step], preferred_element_type=jnp.float32
                    )
                    square = product * product
                    summed = square if summed is None else summed + square
                rounded = summed.astype(jnp.bfloat16).astype(jnp.float32)
                cols = slice(col, col + step)
                if window == 0:
                    o_ref[:, cols] = rounded
                elif window < window_count - 1:
                    o_ref[:, cols] += rounded
                else:
                    o_ref[:, cols] = (o_ref[:, cols] + rounded) / total_tokens

        for count in range(1, MAXDOC + 1):
            pl.when(used == count)(lambda count=count: documents(count))


def owned_squares(lengths, own_rows, other_rows, act_rows, total_tokens):
    window_count, half, row_count = own_rows.shape
    tok_rows, col_count = act_rows.shape[1:]
    tile = row_count // 2
    multiplies = window_count * MAXDOC * tok_rows * row_count * col_count
    return pl.pallas_call(
        lambda *refs: squares_kernel(total_tokens, *refs),
        grid=(row_count // tile,),
        out_shape=jax.ShapeDtypeStruct((row_count, col_count), jnp.float32),
        in_specs=[
            pl.BlockSpec(memory_space=pltpu.SMEM),
            pl.BlockSpec((window_count, half, tile), lambda i: (0, 0, i)),
            pl.BlockSpec((window_count, half, tile), lambda i: (0, 0, i)),
            pl.BlockSpec((window_count, tok_rows, col_count), lambda i: (0, 0, 0)),
        ],
        out_specs=pl.BlockSpec((tile, col_count), lambda i: (i, 0)),
        compiler_params=pltpu.CompilerParams(vmem_limit_bytes=VMEM_LIMIT),
        cost_estimate=pl.CostEstimate(
            flops=2 * multiplies,
            bytes_accessed=4 * row_count * col_count + 4 * window_count * tok_rows * col_count,
            transcendentals=0,
        ),
    )(lengths, own_rows, other_rows, act_rows)


def exchange_kernel(
    dp_count, grads, basis, acts, act_basis, lengths, r_out, a_out, l_out,
    g_buf, b_buf, x_buf, w_buf, part, came, a_all, r_buf, l_buf,
    g_send, g_recv, z_send, z_recv, x_send, x_recv, one_send, one_recv, l_send, l_recv, local,
):
    me = lax.axis_index("dp")
    sub = lax.axis_index("sub")
    mp = lax.axis_index("mp")
    half = g_buf.shape[1]
    mesh_id = pl.DeviceIdType.MESH

    def to_dp(shift):
        return {"dp": lax.rem(me + shift, dp_count)}

    def from_dp(shift):
        return lax.rem(me + dp_count - shift, dp_count)

    to_mp = {"mp": 1 - mp}
    to_sub = {"sub": 1 - sub}

    own_copies = [
        pltpu.make_async_copy(acts, x_buf, local.at[0]),
        pltpu.make_async_copy(act_basis, w_buf, local.at[1]),
        pltpu.make_async_copy(basis, b_buf.at[sub], local.at[2]),
        pltpu.make_async_copy(
            grads.at[pl.ds(sub * half, half), pl.ds(me * BG, BG)], g_buf.at[me], local.at[3]
        ),
        pltpu.make_async_copy(lengths, l_buf.at[me], local.at[4]),
    ]
    for copy in own_copies:
        copy.start()

    barrier = pltpu.get_barrier_semaphore()
    for shift in range(1, dp_count):
        pl.semaphore_signal(barrier, inc=1, device_id=to_dp(shift), device_id_type=mesh_id)
    pl.semaphore_signal(barrier, inc=1, device_id=to_mp, device_id_type=mesh_id)
    pl.semaphore_signal(barrier, inc=1, device_id=to_sub, device_id_type=mesh_id)
    pl.semaphore_wait(barrier, dp_count + 1)

    def remote(src, dst, send, recv, target):
        return pltpu.make_async_remote_copy(
            src_ref=src, dst_ref=dst, send_sem=send, recv_sem=recv,
            device_id=target, device_id_type=mesh_id,
        )

    def grad_copy(shift):
        target = lax.rem(me + shift, dp_count)
        return remote(
            grads.at[pl.ds(sub * half, half), pl.ds(target * BG, BG)], g_buf.at[me],
            g_send.at[shift], g_recv.at[shift], to_dp(shift),
        )

    def grad_arrival(shift):
        return remote(
            g_buf.at[from_dp(shift)], g_buf.at[from_dp(shift)],
            g_send.at[shift], g_recv.at[shift], to_dp(shift),
        )

    basis_copy = remote(basis, b_buf.at[sub], one_send.at[0], one_recv.at[0], to_sub)
    basis_arrival = remote(basis, b_buf.at[1 - sub], one_send.at[0], one_recv.at[0], to_sub)
    grad_copies = [grad_copy(shift) for shift in range(1, dp_count)]
    for copy in grad_copies:
        copy.start()
    basis_copy.start()
    length_copies = [
        remote(lengths, l_buf.at[me], l_send.at[shift], l_recv.at[shift], to_dp(shift))
        for shift in range(1, dp_count)
    ]
    for copy in length_copies:
        copy.start()

    own_copies[0].wait()
    own_copies[1].wait()
    step = 256

    @pl.loop(0, w_buf.shape[1] // step)
    def _(index):
        cols = pl.ds(pl.multiple_of(index * step, step), step)
        product = jnp.dot(x_buf[...], w_buf[:, cols], preferred_element_type=jnp.float32)
        product = product.astype(jnp.bfloat16)
        part[0, :, cols] = product[:half]
        part[1, :, cols] = product[half:]

    share_copy = remote(part.at[1 - mp], came, one_send.at[1], one_recv.at[1], to_mp)
    share_copy.start()

    def rotate(window):
        width = b_buf.shape[2]
        piece = g_buf[window]
        for side in range(2):
            r_buf[window, :, side * width:(side + 1) * width] = jnp.dot(
                piece, b_buf[side], preferred_element_type=jnp.float32
            ).astype(jnp.bfloat16)

    share_copy.wait_recv()
    a_all[me, mp] = (
        part[mp].astype(jnp.float32) + came[...].astype(jnp.float32)
    ).astype(jnp.bfloat16)

    def act_copy(shift):
        return remote(
            a_all.at[me, mp], a_all.at[me, mp], z_send.at[shift], z_recv.at[shift], to_dp(shift)
        )

    def act_arrival(shift):
        window = from_dp(shift)
        return remote(
            a_all.at[window, mp], a_all.at[window, mp], z_send.at[shift], z_recv.at[shift], to_dp(shift)
        )

    def cross_copy(shift):
        window = from_dp(shift)
        return remote(
            a_all.at[window, mp], a_all.at[window, mp], x_send.at[shift], x_recv.at[shift], to_mp
        )

    def cross_arrival(shift):
        window = from_dp(shift)
        return remote(
            a_all.at[window, 1 - mp], a_all.at[window, 1 - mp], x_send.at[shift], x_recv.at[shift], to_mp
        )

    act_copies = [act_copy(shift) for shift in range(1, dp_count)]
    for copy in act_copies:
        copy.start()
    cross_copies = [cross_copy(shift) for shift in range(dp_count)]
    cross_copies[0].start()

    own_copies[2].wait()
    own_copies[3].wait()
    basis_arrival.wait_recv()
    rotate(me)
    for shift in (1, 3, 2):
        grad_arrival(shift).wait_recv()
        rotate(from_dp(shift))
    r_copy = pltpu.make_async_copy(r_buf, r_out, local.at[0])
    r_copy.start()
    own_copies[4].wait()
    for shift in range(1, dp_count):
        window = from_dp(shift)
        remote(
            lengths, l_buf.at[window], l_send.at[shift], l_recv.at[shift], to_dp(shift)
        ).wait_recv()
    l_copy = pltpu.make_async_copy(l_buf, l_out, local.at[2])
    l_copy.start()
    for shift in (1, 3, 2):
        act_arrival(shift).wait_recv()
        cross_copies[shift].start()
    for shift in range(dp_count):
        cross_arrival(shift).wait_recv()
    a_copy = pltpu.make_async_copy(a_all, a_out, local.at[1])
    a_copy.start()
    basis_copy.wait_send()
    share_copy.wait_send()
    for copy in grad_copies + act_copies + cross_copies + length_copies:
        copy.wait_send()
    r_copy.wait()
    a_copy.wait()
    l_copy.wait()


def exchange(activations, grads, act_basis, grad_basis, lengths):
    dp_count = lax.axis_size("dp")
    tok_rows = grads.shape[0]
    half = tok_rows // 2
    width = grad_basis.shape[1]
    cols = act_basis.shape[1]
    anywhere = pl.BlockSpec(memory_space=pl.ANY)
    dma = pltpu.SemaphoreType.DMA
    kind = jnp.bfloat16
    rotated, acts, all_lengths = pl.pallas_call(
        lambda *refs: exchange_kernel(dp_count, *refs),
        out_shape=(
            jax.ShapeDtypeStruct((dp_count, half, 2 * width), kind),
            jax.ShapeDtypeStruct((dp_count, 2, half, cols), kind),
            jax.ShapeDtypeStruct((dp_count,) + lengths.shape, lengths.dtype),
        ),
        in_specs=[anywhere] * 5,
        out_specs=(anywhere, anywhere, anywhere),
        scratch_shapes=[
            pltpu.VMEM((dp_count, half, BG), kind),
            pltpu.VMEM((2, BG, width), kind),
            pltpu.VMEM(activations.shape, kind),
            pltpu.VMEM(act_basis.shape, kind),
            pltpu.VMEM((2, half, cols), kind),
            pltpu.VMEM((half, cols), kind),
            pltpu.VMEM((dp_count, 2, half, cols), kind),
            pltpu.VMEM((dp_count, half, 2 * width), kind),
            pltpu.VMEM((dp_count,) + lengths.shape, lengths.dtype),
            dma((dp_count,)), dma((dp_count,)), dma((dp_count,)), dma((dp_count,)),
            dma((dp_count,)), dma((dp_count,)), dma((2,)), dma((2,)),
            dma((dp_count,)), dma((dp_count,)), dma((5,)),
        ],
        compiler_params=pltpu.CompilerParams(
            collective_id=0, has_side_effects=True, vmem_limit_bytes=VMEM_LIMIT
        ),
        cost_estimate=pl.CostEstimate(flops=7 * 10**9, bytes_accessed=2**25, transcendentals=0),
    )(grads, grad_basis, activations, act_basis, lengths)
    return rotated, acts.reshape(dp_count, tok_rows, cols), all_lengths


def to_owner(block, owners, dp_count):
    orders = list(itertools.permutations(range(dp_count)))
    table = jnp.array(orders, jnp.int32)
    which = jnp.argmax(jnp.all(table == owners[None, :], axis=1)).astype(jnp.int32)
    branches = [
        lambda moved, order=order: lax.ppermute(moved, "dp", [(j, order[j]) for j in range(dp_count)])
        for order in orders
    ]
    return lax.switch(which, branches, block)


def block_shards(activations, grads, act_basis, grad_basis, doc_lengths, owners):
    tok_rows = grads.shape[0]
    dp_count = lax.axis_size("dp")
    padded = jnp.pad(doc_lengths, ((0, 7), (0, 128 - MAXDOC)))
    rotated, act_all, lengths = exchange(activations, grads, act_basis, grad_basis, padded)
    owned = to_owner(rotated, owners, dp_count)
    other = lax.ppermute(owned, "sub", [(0, 1), (1, 0)])
    return owned_squares(lengths, owned, other, act_all, tok_rows * dp_count)


def shards(activations, grads, act_basis, grad_basis, doc_lengths, owners):
    whole_blocks = grad_basis.shape[0] == BG and grads.shape[1] == BG * lax.axis_size("dp")
    pairs = lax.axis_size("mp") == 2 and lax.axis_size("sub") == 2 and lax.axis_size("dp") == 4
    plan = block_shards if whole_blocks and pairs else general_shards
    return plan(activations, grads, act_basis, grad_basis, doc_lengths, owners)


def solution(mesh):
    return jax.shard_map(
        shards,
        mesh=mesh,
        in_specs=(
            P(("parts", "dp"), "mp"),
            P(("parts", "dp"), "mp"),
            P("mp", "sub"),
            P(("mp", "dp"), "sub"),
            P(("parts", "dp"), None),
            P(),
        ),
        out_specs=P(("parts", "mp", "dp"), "sub"),
        check_vma=False,
    )
```

```python
import functools
import itertools

import jax
import jax.numpy as jnp
from jax import lax
from jax.experimental import pallas as pl
from jax.experimental.pallas import tpu as pltpu
from jax.sharding import PartitionSpec as P

BG = 2560
MAXDOC = 4
VMEM_LIMIT = 60 * 2**20


def rotate_piece(grads, running, shard_rows):
    row_count = shard_rows.shape[0]
    block_count = running.shape[1]
    block_of = jnp.arange(row_count, dtype=jnp.int32) // BG
    pieces = []
    for block_index in range(block_count):
        keep_mask = (block_of == block_index).astype(grads.dtype)
        pieces.append(
            jnp.dot(grads * keep_mask[None, :], shard_rows, preferred_element_type=jnp.float32)
        )
    return jnp.stack(pieces, axis=1)


def window_squares(grad_rows, act_rows, slot_ids):
    window_total = jnp.zeros((grad_rows.shape[1], act_rows.shape[1]), jnp.float32)
    for slot_index in range(MAXDOC):
        masked = act_rows * (slot_ids == slot_index).astype(act_rows.dtype)[:, None]
        product = lax.dot_general(
            grad_rows, masked, (((0,), (0,)), ((), ())), preferred_element_type=jnp.float32
        )
        window_total = window_total + product * product
    return window_total


def inverse_of(owners, dp_count):
    owner_ids = jnp.arange(dp_count, dtype=jnp.int32)
    return jnp.sum(
        owner_ids[:, None] * (owners[:, None] == owner_ids[None, :]).astype(jnp.int32), axis=0
    )


def general_shards(activations, grads, act_basis, grad_basis, doc_lengths, owners):
    tok_rows = grads.shape[0]
    block_count = grads.shape[1] // BG
    act_partial = jnp.dot(activations, act_basis, preferred_element_type=jnp.float32)
    act_rot = lax.psum(act_partial.astype(jnp.bfloat16), "mp")
    start_sum = jnp.zeros((tok_rows, block_count, grad_basis.shape[1]), jnp.float32)
    half_rot = rotate_piece(
        grads, start_sum, lax.all_gather(grad_basis, "dp", axis=0, tiled=True)
    ).astype(jnp.bfloat16)
    grad_rot = lax.all_gather(half_rot, "sub", axis=2, tiled=True)
    grad_flat = grad_rot.reshape(tok_rows, block_count * grad_rot.shape[2])
    ends = jnp.cumsum(doc_lengths[0])
    positions = jnp.arange(tok_rows, dtype=jnp.int32)
    doc_slot = jnp.sum((positions[:, None] >= ends[None, :]).astype(jnp.int32), axis=1)
    dp_count = lax.axis_size("dp")
    inverse = inverse_of(owners, dp_count)
    row_block = grad_flat.shape[1] // dp_count
    ordered_cols = jnp.take(grad_flat.reshape(tok_rows, dp_count, row_block), inverse, axis=1)
    ordered_cols = ordered_cols.reshape(tok_rows, dp_count * row_block)
    total_tokens = tok_rows * dp_count
    window_total = window_squares(ordered_cols, act_rot, doc_slot)
    summed = lax.psum_scatter(
        window_total.astype(jnp.bfloat16), "dp", scatter_dimension=0, tiled=True
    ).astype(jnp.float32)
    return summed / total_tokens


def squares_kernel(total_tokens, lengths_ref, own_ref, other_ref, a_ref, o_ref):
    window_count = own_ref.shape[0]
    tok_rows, col_count = a_ref.shape[1:]
    step = 256
    is_first = lax.axis_index("sub") == 0
    token = lax.broadcasted_iota(jnp.int32, (1, tok_rows), 1)
    for window in range(window_count):
        own, other = own_ref[window], other_ref[window]
        rows = jnp.concatenate(
            [jnp.where(is_first, own, other), jnp.where(is_first, other, own)], axis=0
        )
        flipped = rows.T
        lengths = [lengths_ref[window, 0, slot] for slot in range(MAXDOC)]
        ends = [sum(lengths[1:slot + 1], lengths[0]) for slot in range(MAXDOC)]
        used = sum([(length > 0).astype(jnp.int32) for length in lengths[1:]], 1)

        def documents(count):
            pieces = []
            for slot in range(count):
                keep = token < ends[slot]
                if slot:
                    keep = keep & (token >= ends[slot - 1])
                pieces.append(flipped * keep.astype(jnp.float32).astype(flipped.dtype))
            for col in range(0, col_count, step):
                summed = None
                for piece in pieces:
                    product = jnp.dot(
                        piece, a_ref[window, :, col:col + step], preferred_element_type=jnp.float32
                    )
                    square = product * product
                    summed = square if summed is None else summed + square
                rounded = summed.astype(jnp.bfloat16).astype(jnp.float32)
                cols = slice(col, col + step)
                if window == 0:
                    o_ref[:, cols] = rounded
                elif window < window_count - 1:
                    o_ref[:, cols] += rounded
                else:
                    o_ref[:, cols] = (o_ref[:, cols] + rounded) / total_tokens

        for count in range(1, MAXDOC + 1):
            pl.when(used == count)(lambda count=count: documents(count))


def owned_squares(lengths, own_rows, other_rows, act_rows, total_tokens):
    window_count, half, row_count = own_rows.shape
    tok_rows, col_count = act_rows.shape[1:]
    tile = row_count // 2
    multiplies = window_count * MAXDOC * tok_rows * row_count * col_count
    return pl.pallas_call(
        lambda *refs: squares_kernel(total_tokens, *refs),
        grid=(row_count // tile,),
        out_shape=jax.ShapeDtypeStruct((row_count, col_count), jnp.float32),
        in_specs=[
            pl.BlockSpec(memory_space=pltpu.SMEM),
            pl.BlockSpec((window_count, half, tile), lambda i: (0, 0, i)),
            pl.BlockSpec((window_count, half, tile), lambda i: (0, 0, i)),
            pl.BlockSpec((window_count, tok_rows, col_count), lambda i: (0, 0, 0)),
        ],
        out_specs=pl.BlockSpec((tile, col_count), lambda i: (i, 0)),
        compiler_params=pltpu.CompilerParams(vmem_limit_bytes=VMEM_LIMIT),
        cost_estimate=pl.CostEstimate(
            flops=2 * multiplies,
            bytes_accessed=4 * row_count * col_count + 4 * window_count * tok_rows * col_count,
            transcendentals=0,
        ),
    )(lengths, own_rows, other_rows, act_rows)


def exchange_kernel(
    dp_count, grads, basis, acts, act_basis, lengths, r_out, a_out, l_out,
    g_buf, b_buf, x_buf, w_buf, part, came, r_buf, l_buf,
    g_send, g_recv, one_send, one_recv, l_send, l_recv, local,
):
    me = lax.axis_index("dp")
    sub = lax.axis_index("sub")
    mp = lax.axis_index("mp")
    half = g_buf.shape[1]
    mesh_id = pl.DeviceIdType.MESH

    def to_dp(shift):
        return {"dp": lax.rem(me + shift, dp_count)}

    def from_dp(shift):
        return lax.rem(me + dp_count - shift, dp_count)

    to_mp = {"mp": 1 - mp}
    to_sub = {"sub": 1 - sub}

    own_copies = [
        pltpu.make_async_copy(acts, x_buf, local.at[0]),
        pltpu.make_async_copy(act_basis, w_buf, local.at[1]),
        pltpu.make_async_copy(basis, b_buf.at[sub], local.at[2]),
        pltpu.make_async_copy(
            grads.at[pl.ds(sub * half, half), pl.ds(me * BG, BG)], g_buf.at[me], local.at[3]
        ),
        pltpu.make_async_copy(lengths, l_buf.at[me], local.at[4]),
    ]
    for copy in own_copies:
        copy.start()

    barrier = pltpu.get_barrier_semaphore()
    for shift in range(1, dp_count):
        pl.semaphore_signal(barrier, inc=1, device_id=to_dp(shift), device_id_type=mesh_id)
    pl.semaphore_signal(barrier, inc=1, device_id=to_mp, device_id_type=mesh_id)
    pl.semaphore_signal(barrier, inc=1, device_id=to_sub, device_id_type=mesh_id)
    pl.semaphore_wait(barrier, dp_count + 1)

    def remote(src, dst, send, recv, target):
        return pltpu.make_async_remote_copy(
            src_ref=src, dst_ref=dst, send_sem=send, recv_sem=recv,
            device_id=target, device_id_type=mesh_id,
        )

    def grad_copy(shift):
        target = lax.rem(me + shift, dp_count)
        return remote(
            grads.at[pl.ds(sub * half, half), pl.ds(target * BG, BG)], g_buf.at[me],
            g_send.at[shift], g_recv.at[shift], to_dp(shift),
        )

    def grad_arrival(shift):
        return remote(
            g_buf.at[from_dp(shift)], g_buf.at[from_dp(shift)],
            g_send.at[shift], g_recv.at[shift], to_dp(shift),
        )

    basis_copy = remote(basis, b_buf.at[sub], one_send.at[0], one_recv.at[0], to_sub)
    basis_arrival = remote(basis, b_buf.at[1 - sub], one_send.at[0], one_recv.at[0], to_sub)
    grad_copies = [grad_copy(shift) for shift in range(1, dp_count)]
    for copy in grad_copies:
        copy.start()
    basis_copy.start()
    length_copies = [
        remote(lengths, l_buf.at[me], l_send.at[shift], l_recv.at[shift], to_dp(shift))
        for shift in range(1, dp_count)
    ]
    for copy in length_copies:
        copy.start()

    own_copies[0].wait()
    own_copies[1].wait()
    step = 256

    @pl.loop(0, w_buf.shape[1] // step)
    def _(index):
        cols = pl.ds(pl.multiple_of(index * step, step), step)
        product = jnp.dot(x_buf[...], w_buf[:, cols], preferred_element_type=jnp.float32)
        product = product.astype(jnp.bfloat16)
        part[0, :, cols] = product[:half]
        part[1, :, cols] = product[half:]

    share_copy = remote(part.at[1 - mp], came, one_send.at[1], one_recv.at[1], to_mp)
    share_copy.start()

    def rotate(window):
        width = b_buf.shape[2]
        piece = g_buf[window]
        for side in range(2):
            r_buf[window, :, side * width:(side + 1) * width] = jnp.dot(
                piece, b_buf[side], preferred_element_type=jnp.float32
            ).astype(jnp.bfloat16)

    own_copies[2].wait()
    own_copies[3].wait()
    basis_arrival.wait_recv()
    rotate(me)
    share_copy.wait_recv()
    came[...] = (
        part[mp].astype(jnp.float32) + came[...].astype(jnp.float32)
    ).astype(jnp.bfloat16)
    a_copy = pltpu.make_async_copy(came, a_out, local.at[1])
    a_copy.start()
    for shift in (1, 3, 2):
        grad_arrival(shift).wait_recv()
        rotate(from_dp(shift))
    r_copy = pltpu.make_async_copy(r_buf, r_out, local.at[0])
    r_copy.start()
    own_copies[4].wait()
    for shift in range(1, dp_count):
        window = from_dp(shift)
        remote(
            lengths, l_buf.at[window], l_send.at[shift], l_recv.at[shift], to_dp(shift)
        ).wait_recv()
    l_copy = pltpu.make_async_copy(l_buf, l_out, local.at[2])
    l_copy.start()
    basis_copy.wait_send()
    share_copy.wait_send()
    for copy in grad_copies + length_copies:
        copy.wait_send()
    r_copy.wait()
    a_copy.wait()
    l_copy.wait()


def exchange(activations, grads, act_basis, grad_basis, lengths):
    dp_count = lax.axis_size("dp")
    tok_rows = grads.shape[0]
    half = tok_rows // 2
    width = grad_basis.shape[1]
    cols = act_basis.shape[1]
    anywhere = pl.BlockSpec(memory_space=pl.ANY)
    dma = pltpu.SemaphoreType.DMA
    kind = jnp.bfloat16
    return pl.pallas_call(
        lambda *refs: exchange_kernel(dp_count, *refs),
        out_shape=(
            jax.ShapeDtypeStruct((dp_count, half, 2 * width), kind),
            jax.ShapeDtypeStruct((half, cols), kind),
            jax.ShapeDtypeStruct((dp_count,) + lengths.shape, lengths.dtype),
        ),
        in_specs=[anywhere] * 5,
        out_specs=(anywhere, anywhere, anywhere),
        scratch_shapes=[
            pltpu.VMEM((dp_count, half, BG), kind),
            pltpu.VMEM((2, BG, width), kind),
            pltpu.VMEM(activations.shape, kind),
            pltpu.VMEM(act_basis.shape, kind),
            pltpu.VMEM((2, half, cols), kind),
            pltpu.VMEM((half, cols), kind),
            pltpu.VMEM((dp_count, half, 2 * width), kind),
            pltpu.VMEM((dp_count,) + lengths.shape, lengths.dtype),
            dma((dp_count,)), dma((dp_count,)), dma((2,)), dma((2,)),
            dma((dp_count,)), dma((dp_count,)), dma((5,)),
        ],
        compiler_params=pltpu.CompilerParams(
            collective_id=0, has_side_effects=True, vmem_limit_bytes=VMEM_LIMIT
        ),
        cost_estimate=pl.CostEstimate(flops=7 * 10**9, bytes_accessed=2**25, transcendentals=0),
    )(grads, grad_basis, activations, act_basis, lengths)


def share_kernel(
    dp_count, share, a_out, a_all, z_send, z_recv, x_send, x_recv, local
):
    me = lax.axis_index("dp")
    mp = lax.axis_index("mp")
    mesh_id = pl.DeviceIdType.MESH
    to_mp = {"mp": 1 - mp}
    own = pltpu.make_async_copy(share, a_all.at[me, mp], local.at[0])
    own.start()

    def to_dp(shift):
        return {"dp": lax.rem(me + shift, dp_count)}

    barrier = pltpu.get_barrier_semaphore()
    for shift in range(1, dp_count):
        pl.semaphore_signal(barrier, inc=1, device_id=to_dp(shift), device_id_type=mesh_id)
    pl.semaphore_signal(barrier, inc=1, device_id=to_mp, device_id_type=mesh_id)
    pl.semaphore_wait(barrier, dp_count)

    def window(shift):
        return lax.rem(me + dp_count - shift, dp_count)

    def remote(src, dst, send, recv, target):
        return pltpu.make_async_remote_copy(
            src_ref=src, dst_ref=dst, send_sem=send, recv_sem=recv,
            device_id=target, device_id_type=mesh_id,
        )

    sent = [
        remote(share, a_all.at[me, mp], z_send.at[shift], z_recv.at[shift], to_dp(shift))
        for shift in range(1, dp_count)
    ]
    crossed = [remote(share, a_all.at[me, mp], x_send.at[0], x_recv.at[0], to_mp)]
    for copy in sent + crossed:
        copy.start()
    for shift in (1, 3, 2):
        place = a_all.at[window(shift), mp]
        remote(share, place, z_send.at[shift], z_recv.at[shift], to_dp(shift)).wait_recv()
        copy = remote(place, place, x_send.at[shift], x_recv.at[shift], to_mp)
        copy.start()
        crossed.append(copy)
    for shift in range(dp_count):
        place = a_all.at[window(shift), 1 - mp]
        remote(share, place, x_send.at[shift], x_recv.at[shift], to_mp).wait_recv()
    own.wait()
    out = pltpu.make_async_copy(a_all, a_out, local.at[1])
    out.start()
    for copy in sent + crossed:
        copy.wait_send()
    out.wait()


def gather_share(share):
    dp_count = lax.axis_size("dp")
    half, cols = share.shape
    anywhere = pl.BlockSpec(memory_space=pl.ANY)
    dma = pltpu.SemaphoreType.DMA
    shape = (dp_count, 2, half, cols)
    acts = pl.pallas_call(
        lambda *refs: share_kernel(dp_count, *refs),
        out_shape=jax.ShapeDtypeStruct(shape, share.dtype),
        in_specs=[anywhere],
        out_specs=anywhere,
        scratch_shapes=[
            pltpu.VMEM(shape, share.dtype),
            dma((dp_count,)), dma((dp_count,)), dma((dp_count,)), dma((dp_count,)), dma((2,)),
        ],
        compiler_params=pltpu.CompilerParams(
            collective_id=1, has_side_effects=True, vmem_limit_bytes=VMEM_LIMIT
        ),
        cost_estimate=pl.CostEstimate(flops=10**7, bytes_accessed=10**7, transcendentals=0),
    )(share)
    return acts.reshape(dp_count, 2 * half, cols)


def to_owner(block, share, owners, dp_count):
    orders = list(itertools.permutations(range(dp_count)))
    table = jnp.array(orders, jnp.int32)
    which = jnp.argmax(jnp.all(table == owners[None, :], axis=1)).astype(jnp.int32)

    def move(order, moved, shared):
        moved = lax.ppermute(moved, "dp", [(j, order[j]) for j in range(dp_count)])
        return moved, gather_share(shared)

    branches = [functools.partial(move, order) for order in orders]
    return lax.switch(which, branches, block, share)


def block_shards(activations, grads, act_basis, grad_basis, doc_lengths, owners):
    tok_rows = grads.shape[0]
    dp_count = lax.axis_size("dp")
    padded = jnp.pad(doc_lengths, ((0, 7), (0, 128 - MAXDOC)))
    rotated, share, lengths = exchange(activations, grads, act_basis, grad_basis, padded)
    owned, act_all = to_owner(rotated, share, owners, dp_count)
    other = lax.ppermute(owned, "sub", [(0, 1), (1, 0)])
    return owned_squares(lengths, owned, other, act_all, tok_rows * dp_count)


def shards(activations, grads, act_basis, grad_basis, doc_lengths, owners):
    whole_blocks = grad_basis.shape[0] == BG and grads.shape[1] == BG * lax.axis_size("dp")
    pairs = lax.axis_size("mp") == 2 and lax.axis_size("sub") == 2 and lax.axis_size("dp") == 4
    plan = block_shards if whole_blocks and pairs else general_shards
    return plan(activations, grads, act_basis, grad_basis, doc_lengths, owners)


def solution(mesh):
    return jax.shard_map(
        shards,
        mesh=mesh,
        in_specs=(
            P(("parts", "dp"), "mp"),
            P(("parts", "dp"), "mp"),
            P("mp", "sub"),
            P(("mp", "dp"), "sub"),
            P(("parts", "dp"), None),
            P(),
        ),
        out_specs=P(("parts", "mp", "dp"), "sub"),
        check_vma=False,
    )
```
